32 devices in a mesh: mut: 8 (over z, core), test: 4 (over y, x).
Axes of the slice: x: 2, y: 2, z: 4, core: 2. Of those that a mesh axis runs over, the one named last changes fastest.
Arguments:
- input_activation: bfloat16 [128, 28, 1024], P(('mut', 'test')), may hold values from -18 to 18
- ground_truth_class: int32 [128], replicated, may hold values from 0 to 999
- remaining_pictures: int32 [32, 56], P('mut', 'test'), may hold values from 0 to 31, as said below
- learned_narrowing_kernel: bfloat16 [1024, 256], replicated, may hold values from -0.1875 to 0.1875
- learned_widening_kernel: bfloat16 [256, 1024], replicated, may hold values from -0.375 to 0.375
- narrowing_perturbation: bfloat16 [32, 1024, 256], P('mut', 'test'), may hold values from -0.09375 to 0.09375
- widening_perturbation: bfloat16 [32, 256, 1024], P('mut', None, 'test'), may hold values from -0.1875 to 0.1875
- perturbation_strength: float32 [32, 2], P('mut'), may hold values from 0.25 to 2
- readout_matrix: bfloat16 [1024, 1000], replicated, may hold values from -1 to 1
Outputs:
- kill: float32 [32, 2, 56], P('mut', None, 'test')
The draws below stay inside these ranges and needn't reach their ends.
Inputs may be any that keep to these rules, and one draw needn't show every extreme that they name: `remaining_pictures`: entry t * 14 + j of a mutant's row names an image of test shard t; image i of a shard lies on the device at mut index i // 4. Among the entries of one mut index's 4 mutants in one test shard, at most 10 lie on any one device's images, and some device takes exactly 10.
All inputs are finite; a program needn't handle non-finite values.
Results may differ from the reference program's by a relative error of at most 0.0003.
Values may be sent and summed in bfloat16 or wider, within the bound.
A program may use at most 64 MiB of HBM per device.

```python
import math
import jax
import jax.numpy as jnp
from jax import lax

C = 1024
B = 256
CLASSES = 1000
PIX = 28
STEPS = 2
IMG_DEV = 4
MUT_DEV = 4
SURV = 14
IMAGES = 128
MUTANTS = 32
SURV_ALL = 56
CAP = 10


def draw_remaining_pictures(key, part):
    n_mut = MUTANTS // MUT_DEV
    n_test = SURV_ALL // SURV
    wanted = MUT_DEV * SURV
    pool_size = n_mut * CAP

    def one_group(group_key):
        key_a, key_b, key_c = jax.random.split(group_key, 3)
        perm = jax.random.permutation(key_a, pool_size)
        pool = perm // CAP
        position = jnp.arange(pool_size, dtype=jnp.int32)
        order_key = jnp.where(pool == pool[0], position - pool_size, position)
        ordered = pool[jnp.argsort(order_key, stable=True)][:wanted]
        ordered = ordered[jax.random.permutation(key_b, wanted)]
        within = jax.random.randint(key_c, (wanted,), 0, IMG_DEV)
        return (ordered * IMG_DEV + within).astype(jnp.int32)
    keys = jax.random.split(jax.random.fold_in(key, 11), n_mut * n_test)
    table = jax.vmap(one_group)(keys)
    table = table.reshape(n_mut, n_test, MUT_DEV, SURV)
    table = jnp.transpose(table, (0, 2, 1, 3))
    return table.reshape(MUTANTS, SURV_ALL).astype(jnp.int32)


def draw_input_activation(key, part):
    key_a = jax.random.fold_in(jax.random.fold_in(key, 23), 0)
    values = jax.random.normal(key_a, (IMAGES, PIX, C), jnp.float32)
    return jnp.clip(values, -6.0, 6.0).astype(jnp.bfloat16)


def draw_readout_matrix(key, part):
    key_a = jax.random.fold_in(jax.random.fold_in(key, 37), 0)
    values = jax.random.normal(key_a, (C, CLASSES), jnp.float32) * (1.0 / math.sqrt(C))
    return jnp.clip(values, -1.0, 1.0).astype(jnp.bfloat16)


def place_ends(result, rng, smallest, largest):
    spot = [jax.random.randint(jax.random.fold_in(rng, axis), (), 0, length) for axis, length in enumerate(result.shape)]
    longest = result.shape.index(max(result.shape))
    neighbour = spot[:longest] + [(spot[longest] + 1) % result.shape[longest]] + spot[longest + 1:]
    return result.at[tuple(spot)].set(smallest).at[tuple(neighbour)].set(largest)


def levels(stream_key, extent, cuts, least, largest):
    gain = 1.0
    for dim, shards_of in cuts:
        heights = jax.random.uniform(jax.random.fold_in(jax.random.fold_in(stream_key, 6), dim), (shards_of,), jnp.float32, least / len(cuts), largest / len(cuts))
        gain = gain * jnp.repeat(jnp.exp(heights), extent[dim] // shards_of).reshape((-1,) + (1,) * (len(extent) - 1 - dim))
    return gain


def gaussian(key, shape, spread, limit, cuts=(), held_as=jnp.bfloat16):
    values = jax.random.normal(key, shape, jnp.float32) * spread
    if len(cuts) > 0:
        values = levels(key, shape, cuts, -0.22, 0.18) * values
    return jnp.clip(values, min=-limit, max=limit).astype(held_as)


def setup_inputs(seed: int = 0) -> dict:
    key_list = jax.random.split(jax.random.key(seed), 10)
    return {
        "input_activation": draw_input_activation(jax.random.fold_in(key_list[9], 71), 0),
        "ground_truth_class": place_ends(jax.random.randint(key_list[1], (IMAGES,), 0, CLASSES), jax.random.fold_in(key_list[1], 1), 0, CLASSES - 1).astype(jnp.int32),
        "remaining_pictures": draw_remaining_pictures(jax.random.fold_in(key_list[9], 71), 0),
        "learned_narrowing_kernel": gaussian(key_list[3], (C, B), C ** -0.5, 0.1875),
        "learned_widening_kernel": gaussian(key_list[4], (B, C), B ** -0.5, 0.375),
        "narrowing_perturbation": gaussian(key_list[5], (MUTANTS, C, B), (4 * C) ** -0.5, 0.09375, ((0, 8), (1, 4))),
        "widening_perturbation": gaussian(key_list[6], (MUTANTS, B, C), (4 * B) ** -0.5, 0.1875, ((0, 8), (2, 4))),
        "perturbation_strength": jnp.clip(jnp.exp(math.log(2.0) - 2.0794415 * jax.random.uniform(key_list[7], (MUTANTS, STEPS), jnp.float32) ** levels(key_list[7], (MUTANTS, STEPS), ((0, 8),), -0.2, 0.2)), 0.25, 2.0),
        "readout_matrix": draw_readout_matrix(jax.random.fold_in(key_list[9], 71), 0),
    }


def evaluate(x_block, target_class_slice, mags, d_first, d_last, learned_narrowing_kernel, learned_widening_kernel, readout_matrix):
    rows = x_block.reshape(-1, x_block.shape[2])
    kills = []
    for step in range(STEPS):
        w_first = (learned_narrowing_kernel.astype(jnp.float32) + mags[step] * d_first.astype(jnp.float32)).astype(jnp.bfloat16)
        w_last = (learned_widening_kernel.astype(jnp.float32) + mags[step] * d_last.astype(jnp.float32)).astype(jnp.bfloat16)
        hidden = jnp.maximum(jnp.dot(rows, w_first, preferred_element_type=jnp.float32), 0.0).astype(jnp.bfloat16)
        out_rows = jnp.maximum(jnp.dot(hidden, w_last, preferred_element_type=jnp.float32) + rows.astype(jnp.float32), 0.0)
        pooled = jnp.mean(out_rows.reshape(x_block.shape), axis=1).astype(jnp.bfloat16)
        logits = jnp.dot(pooled, readout_matrix, preferred_element_type=jnp.float32)
        top = jnp.max(logits, axis=1, keepdims=True)
        total = top[:, 0] + jnp.log(jnp.sum(jnp.exp(logits - top), axis=1))
        column = jnp.arange(logits.shape[1], dtype=jnp.int32)
        selected_entries = jnp.sum(jnp.where(column[None, :] == target_class_slice[:, None], logits, 0.0), axis=1)
        kills.append(total - selected_entries)
    return jnp.stack(kills)


def reference(input_activation, ground_truth_class, remaining_pictures, learned_narrowing_kernel, learned_widening_kernel, narrowing_perturbation, widening_perturbation, perturbation_strength, readout_matrix):
    n_test = SURV_ALL // SURV
    shard = (jnp.arange(SURV_ALL, dtype=jnp.int32) // SURV).astype(jnp.int32)

    def one_mutant(variant_number):
        killing_tally = remaining_pictures[variant_number]
        whole = (((killing_tally // IMG_DEV) * n_test + shard) * IMG_DEV + killing_tally % IMG_DEV).astype(jnp.int32)
        x_block = jnp.take(input_activation, whole, axis=0)
        target_class_slice = jnp.take(ground_truth_class, whole)
        return evaluate(x_block, target_class_slice, perturbation_strength[variant_number], narrowing_perturbation[variant_number], widening_perturbation[variant_number], learned_narrowing_kernel, learned_widening_kernel, readout_matrix)

    return lax.map(one_mutant, jnp.arange(MUTANTS, dtype=jnp.int32))
```

```python
import functools

import jax
import jax.numpy as jnp
from jax import lax
from jax.experimental import pallas as pl
from jax.experimental.pallas import tpu as pltpu
from jax.sharding import PartitionSpec as P

MESH = pl.DeviceIdType.MESH
F32, BF16 = jnp.float32, jnp.bfloat16


def round_up(value, unit):
    return (value + unit - 1) // unit * unit


def kernel(
    n_mut,
    n_test,
    left_ref,
    strength_ref,
    label_ref,
    x_ref,
    d1_ref,
    d2_ref,
    w1_ref,
    w2_ref,
    readout_ref,
    kill_ref,
    images,
    d1_all,
    d2_all,
    w1,
    w2,
    readout,
    rows,
    w1_step,
    pooled,
    labels,
    local_sem,
    x_send,
    x_recv,
    sib_send,
    sib_recv,
    d_send,
    d_recv,
):
    img_dev, pix, width = x_ref.shape
    slot = images.shape[1]
    n_var, surv = left_ref.shape
    steps = strength_ref.shape[1]
    block = d1_ref.shape[1]
    narrow = d1_ref.shape[2]
    padded = pooled.shape[1]
    m, t = lax.axis_index("mut"), lax.axis_index("test")
    chips = n_mut // 2
    sibling = m + 1 - 2 * (m % 2)
    far = [(m + 2 * k) % n_mut for k in range(1, chips)]
    far_from = [(m + n_mut - 2 * k) % n_mut for k in range(1, chips)]
    square = n_test == 4
    if square:
        across, along = t + 1 - 2 * (t % 2), (t + 2) % 4
        near = [across, along]
        origin = [across, along, 3 - t]
    else:
        near = [(t + k) % n_test for k in range(1, n_test)]
        origin = [(t + n_test - k) % n_test for k in range(1, n_test)]

    local = [
        pltpu.make_async_copy(w1_ref, w1, local_sem.at[0]),
        pltpu.make_async_copy(w2_ref, w2, local_sem.at[1]),
        pltpu.make_async_copy(readout_ref, readout, local_sem.at[2]),
        pltpu.make_async_copy(d1_ref, d1_all.at[:, t], local_sem.at[3]),
        pltpu.make_async_copy(d2_ref, d2_all.at[:, t], local_sem.at[4]),
    ]

    barrier = pltpu.get_barrier_semaphore()
    for peer in [sibling] + far:
        pl.semaphore_signal(barrier, inc=1, device_id=(peer, t), device_id_type=MESH)
    for peer in near:
        pl.semaphore_signal(barrier, inc=1, device_id=(m, peer), device_id_type=MESH)
    for copy in local:
        copy.start()
    images[pl.ds(m * img_dev, img_dev)] = jnp.concatenate(
        [x_ref[...], jnp.zeros((img_dev, slot - pix, width), BF16)], axis=1
    )
    pl.semaphore_wait(barrier, 1 + len(far) + len(near))

    def x_copy(source, send, recv, target):
        view = images.at[pl.ds(source * img_dev, img_dev)]
        return pltpu.make_async_remote_copy(
            view, view, send, recv, device_id=(target, t), device_id_type=MESH
        )

    def own_copy(which, i, place):
        ref, full = ((d1_ref, d1_all), (d2_ref, d2_all))[which]
        return pltpu.make_async_remote_copy(
            ref.at[i],
            full.at[i, t],
            d_send.at[which, i, place],
            d_recv.at[which, i, place],
            device_id=(m, near[place]),
            device_id_type=MESH,
        )

    def held_copy(which, i, place, target):
        view = (d1_all, d2_all)[which].at[i, origin[place]]
        return pltpu.make_async_remote_copy(
            view,
            view,
            d_send.at[which, i, 2],
            d_recv.at[which, i, 2],
            device_id=(m, target),
            device_id_type=MESH,
        )

    def arrived(which, i, place):
        view = (d1_all, d2_all)[which].at[i, origin[place]]
        pltpu.make_async_remote_copy(
            view,
            view,
            d_send.at[which, i, place],
            d_recv.at[which, i, place],
            device_id=(m, near[0]),
            device_id_type=MESH,
        ).wait_recv()

    def send_own(i):
        for which in range(2):
            for place in range(len(near)):
                own_copy(which, i, place).start()

    def pass_on(i):
        if square:
            arrived(0, i, 0)
            held_copy(0, i, 0, along).start()
            arrived(1, i, 1)
            held_copy(1, i, 1, across).start()

    x_out = [x_copy(m, x_send.at[k], x_recv.at[k], far[k]) for k in range(chips - 1)]
    sib_out = [x_copy(m, sib_send.at[0], sib_recv.at[0], sibling)]
    for copy in x_out:
        copy.start()
    send_own(0)
    send_own(1)
    sib_out[0].start()
    pass_on(0)
    for i in range(2, n_var):
        send_own(i)
    pass_on(1)
    for k in range(chips - 1):
        x_copy(far_from[k], x_send.at[k], x_recv.at[k], far[k]).wait_recv()
        copy = x_copy(far_from[k], sib_send.at[k + 1], sib_recv.at[k + 1], sibling)
        copy.start()
        sib_out.append(copy)
    sib_from = [sibling] + [(sibling + n_mut - 2 * k) % n_mut for k in range(1, chips)]
    for k in range(chips):
        x_copy(sib_from[k], sib_send.at[k], sib_recv.at[k], sibling).wait_recv()
    for copy in local:
        copy.wait()

    def variant(i, carry):
        for place in range(len(origin)):
            for which in range(2):
                if not (square and place == which):
                    arrived(which, i, place)
        for j in range(surv):
            entry = left_ref[i, j]
            rows[pl.ds(j * slot, slot), :] = images[entry]
            number = (entry // img_dev * n_test + t) * img_dev + entry % img_dev
            labels[i, pl.ds(j, 1), :] = jnp.full((1, 128), label_ref[number], jnp.int32)
        for step in range(steps):
            strength = strength_ref[i, step]
            for part in range(n_test):
                span = pl.ds(part * block, block)
                w1_step[span, :] = (
                    w1[span, :].astype(F32) + strength * d1_all[i, part].astype(F32)
                ).astype(BF16)
            hidden = jnp.maximum(
                jnp.dot(rows[...], w1_step[...], preferred_element_type=F32), 0.0
            ).astype(BF16)
            for part in range(n_test):
                span = pl.ds(part * block, block)
                w2_step = (
                    w2[:, span].astype(F32) + strength * d2_all[i, part].astype(F32)
                ).astype(BF16)
                out = jnp.maximum(
                    jnp.dot(hidden, w2_step, preferred_element_type=F32)
                    + rows[:, span].astype(F32),
                    0.0,
                )
                mean = jnp.sum(out.reshape(surv, slot, block), axis=1) * (1.0 / pix)
                pooled[i * steps + step, :, span] = jnp.concatenate(
                    [mean, jnp.zeros((padded - surv, block), F32)], axis=0
                ).astype(BF16)
        if square:

            @pl.when(i + 2 < n_var)
            def _():
                pass_on(i + 2)

        return carry

    lax.fori_loop(0, n_var, variant, 0)

    count = n_var * steps * padded
    logits = jnp.dot(
        pooled[...].reshape(count, width), readout[...], preferred_element_type=F32
    )
    classes = logits.shape[1]
    top = jnp.max(logits, axis=1, keepdims=True)
    total = top + jnp.log(jnp.sum(jnp.exp(logits - top), axis=1, keepdims=True))
    wanted = jnp.concatenate(
        [labels[i // steps][:, 0:1] for i in range(n_var * steps)], axis=0
    )
    column = lax.broadcasted_iota(jnp.int32, (count, classes), 1)
    chosen = jnp.sum(jnp.where(column == wanted, logits, 0.0), axis=1, keepdims=True)
    kill = total - chosen
    row = lax.broadcasted_iota(jnp.int32, (count, 128), 0) % padded
    lane = lax.broadcasted_iota(jnp.int32, (count, 128), 1)
    spread = jnp.sum(
        jnp.where(row == lane, kill, 0.0).reshape(n_var * steps, padded, 128), axis=1
    )
    for i in range(n_var):
        kill_ref[i] = spread[i * steps : (i + 1) * steps, :surv]

    for copy in x_out + sib_out:
        copy.wait_send()

    def drain(i, carry):
        for which in range(2):
            for place in range(len(near)):
                own_copy(which, i, place).wait_send()
        if square:
            held_copy(0, i, 0, along).wait_send()
            held_copy(1, i, 1, across).wait_send()
        return carry

    lax.fori_loop(0, n_var, drain, 0)


def solution(mesh):
    n_mut, n_test = mesh.shape["mut"], mesh.shape["test"]

    def on_device(x, label, left, w1, w2, d1, d2, strength, readout):
        img_dev, pix, width = x.shape
        n_var, surv = left.shape
        steps = strength.shape[1]
        block, narrow = d1.shape[1], d1.shape[2]
        slot = round_up(pix, 16)
        padded = round_up(surv, 16)
        dma = pltpu.SemaphoreType.DMA
        places = max(3, n_test - 1)
        chips = n_mut // 2
        smem = pl.BlockSpec(memory_space=pltpu.SMEM)
        vmem = pl.BlockSpec(memory_space=pltpu.VMEM)
        anywhere = pl.BlockSpec(memory_space=pl.ANY)
        macs = n_var * steps * surv * slot * width * narrow * 2
        return pl.pallas_call(
            functools.partial(kernel, n_mut, n_test),
            out_shape=jax.ShapeDtypeStruct((n_var, steps, surv), F32),
            in_specs=[smem, smem, smem, vmem] + [anywhere] * 5,
            out_specs=vmem,
            scratch_shapes=[
                pltpu.VMEM((n_mut * img_dev, slot, width), BF16),
                pltpu.VMEM((n_var, n_test, block, narrow), BF16),
                pltpu.VMEM((n_var, n_test, narrow, block), BF16),
                pltpu.VMEM(w1.shape, BF16),
                pltpu.VMEM(w2.shape, BF16),
                pltpu.VMEM(readout.shape, BF16),
                pltpu.VMEM((surv * slot, width), BF16),
                pltpu.VMEM((width, narrow), BF16),
                pltpu.VMEM((n_var * steps, padded, width), BF16),
                pltpu.VMEM((n_var, padded, 128), jnp.int32),
                dma((5,)),
                dma((chips,)),
                dma((chips,)),
                dma((chips,)),
                dma((chips,)),
                dma((2, n_var, places)),
                dma((2, n_var, places)),
            ],
            compiler_params=pltpu.CompilerParams(
                collective_id=0, has_side_effects=True, vmem_limit_bytes=48 * 2**20
            ),
            cost_estimate=pl.CostEstimate(
                flops=2 * macs, bytes_accessed=8 * 2**20, transcendentals=0
            ),
        )(left, strength, label, x, d1, d2, w1, w2, readout)

    return jax.shard_map(
        on_device,
        mesh=mesh,
        in_specs=(
            P(("mut", "test"), None, None),
            P(),
            P("mut", "test"),
            P(),
            P(),
            P("mut", "test", None),
            P("mut", None, "test"),
            P("mut", None),
            P(),
        ),
        out_specs=P("mut", None, "test"),
        check_vma=False,
    )
```

```python
import functools

import jax
import jax.numpy as jnp
from jax import lax
from jax.experimental import pallas as pl
from jax.experimental.pallas import tpu as pltpu
from jax.sharding import PartitionSpec as P

MESH = pl.DeviceIdType.MESH
F32, BF16 = jnp.float32, jnp.bfloat16


def round_up(value, unit):
    return (value + unit - 1) // unit * unit


def kernel(
    n_mut,
    n_test,
    left_ref,
    strength_ref,
    label_ref,
    x_ref,
    d1_ref,
    d2_ref,
    w1_ref,
    w2_ref,
    readout_ref,
    kill_ref,
    images,
    d1_all,
    d2_all,
    w1,
    w2,
    readout,
    rows,
    w1_step,
    pooled,
    labels,
    local_sem,
    x_send,
    x_recv,
    sib_send,
    sib_recv,
    d_send,
    d_recv,
):
    pix, img_dev, width = x_ref.shape
    slot = images.shape[1]
    n_var, surv = left_ref.shape
    steps = strength_ref.shape[0]
    block = d1_ref.shape[1]
    narrow = d1_ref.shape[2]
    padded = pooled.shape[1]
    m, t = lax.axis_index("mut"), lax.axis_index("test")
    chips = n_mut // 2
    sibling = m + 1 - 2 * (m % 2)
    chip = m // 2
    square = n_test == 4
    if square:
        across, along = t + 1 - 2 * (t % 2), (t + 2) % 4
        near = [across, along]
        origin = [across, along, 3 - t]
    else:
        near = [(t + k) % n_test for k in range(1, n_test)]
        origin = [(t + n_test - k) % n_test for k in range(1, n_test)]

    def reaches(sign, k):
        return chip + k < chips if sign > 0 else chip >= k

    local = [
        pltpu.make_async_copy(w1_ref, w1, local_sem.at[0]),
        pltpu.make_async_copy(w2_ref, w2, local_sem.at[1]),
        pltpu.make_async_copy(readout_ref, readout, local_sem.at[2]),
        pltpu.make_async_copy(d1_ref, d1_all.at[:, t], local_sem.at[3]),
        pltpu.make_async_copy(d2_ref, d2_all.at[:, t], local_sem.at[4]),
    ]

    barrier = pltpu.get_barrier_semaphore()
    pl.semaphore_signal(barrier, inc=1, device_id=(sibling, t), device_id_type=MESH)
    for sign in (1, -1):

        @pl.when(reaches(sign, 1))
        def _():
            pl.semaphore_signal(
                barrier, inc=1, device_id=(m + 2 * sign, t), device_id_type=MESH
            )

    for peer in near:
        pl.semaphore_signal(barrier, inc=1, device_id=(m, peer), device_id_type=MESH)
    for copy in local:
        copy.start()
    for j in range(img_dev):
        images[m * img_dev + j] = jnp.concatenate(
            [x_ref[:, j, :], jnp.zeros((slot - pix, width), BF16)], axis=0
        )
    below = (chip + chips - 1) // chips
    above = (2 * chips - 2 - chip) // chips
    pl.semaphore_wait(barrier, 1 + len(near) + below + above)

    def x_copy(source, send, recv, target):
        view = images.at[pl.ds(source * img_dev, img_dev)]
        return pltpu.make_async_remote_copy(
            view, view, send, recv, device_id=(target, t), device_id_type=MESH
        )

    def own_copy(which, i, place):
        ref, full = ((d1_ref, d1_all), (d2_ref, d2_all))[which]
        return pltpu.make_async_remote_copy(
            ref.at[i],
            full.at[i, t],
            d_send.at[which, i, place],
            d_recv.at[which, i, place],
            device_id=(m, near[place]),
            device_id_type=MESH,
        )

    def held_copy(which, i, place, target):
        view = (d1_all, d2_all)[which].at[i, origin[place]]
        return pltpu.make_async_remote_copy(
            view,
            view,
            d_send.at[which, i, 2],
            d_recv.at[which, i, 2],
            device_id=(m, target),
            device_id_type=MESH,
        )

    def arrived(which, i, place):
        view = (d1_all, d2_all)[which].at[i, origin[place]]
        pltpu.make_async_remote_copy(
            view,
            view,
            d_send.at[which, i, place],
            d_recv.at[which, i, place],
            device_id=(m, near[0]),
            device_id_type=MESH,
        ).wait_recv()

    def send_own(i):
        for which in range(2):
            for place in range(len(near)):
                own_copy(which, i, place).start()

    def pass_on(i):
        if square:
            arrived(0, i, 0)
            held_copy(0, i, 0, along).start()
            arrived(1, i, 1)
            held_copy(1, i, 1, across).start()

    def hop(sign, k):
        way = (1 - sign) // 2
        return x_copy(
            m - 2 * sign * k, x_send.at[way, k], x_recv.at[way, k + 1], m + 2 * sign
        )

    def landed(sign, k):
        way = (1 - sign) // 2
        return x_copy(
            m - 2 * sign * k, x_send.at[way, k], x_recv.at[way, k], m + 2 * sign
        )

    def hand_over(sign, k):
        way = (1 - sign) // 2
        return x_copy(
            m - 2 * sign * k, sib_send.at[way, k], sib_recv.at[way, k], sibling
        )

    def handed(sign, k):
        way = (1 - sign) // 2
        return x_copy(
            sibling - 2 * sign * k, sib_send.at[way, k], sib_recv.at[way, k], sibling
        )

    def relay(k):
        for sign in (1, -1):

            @pl.when(reaches(-sign, k))
            def _():
                if k > 0:
                    landed(sign, k).wait_recv()
                if k + 1 < chips:

                    @pl.when(reaches(sign, 1))
                    def _():
                        hop(sign, k).start()

                if k > 0:
                    hand_over(sign, k).start()

    relay(0)
    hand_over(1, 0).start()
    send_own(0)
    send_own(1)
    relay(1)
    pass_on(0)
    for i in range(2, n_var):
        send_own(i)
    for k in range(2, chips):
        relay(k)
        if k < 4:
            pass_on(k - 1)
    handed(1, 0).wait_recv()
    for k in range(1, chips):
        for sign in (1, -1):

            @pl.when(reaches(-sign, k))
            def _():
                handed(sign, k).wait_recv()

    for copy in local:
        copy.wait()

    def variant(i, carry):
        for place in range(len(origin)):
            for which in range(2):
                if not (square and place == which):
                    arrived(which, i, place)
        for j in range(surv):
            entry = left_ref[i, j]
            rows[pl.ds(j * slot, slot), :] = images[entry]
            number = (entry // img_dev * n_test + t) * img_dev + entry % img_dev
            labels[i, pl.ds(j, 1), :] = jnp.full((1, 128), label_ref[number], jnp.int32)
        for step in range(steps):
            strength = strength_ref[step, i]
            for part in range(n_test):
                span = pl.ds(part * block, block)
                w1_step[span, :] = (
                    w1[span, :].astype(F32) + strength * d1_all[i, part].astype(F32)
                ).astype(BF16)
            hidden = jnp.maximum(
                jnp.dot(rows[...], w1_step[...], preferred_element_type=F32), 0.0
            ).astype(BF16)
            for part in range(n_test):
                span = pl.ds(part * block, block)
                w2_step = (
                    w2[:, span].astype(F32) + strength * d2_all[i, part].astype(F32)
                ).astype(BF16)
                out = jnp.maximum(
                    jnp.dot(hidden, w2_step, preferred_element_type=F32)
                    + rows[:, span].astype(F32),
                    0.0,
                )
                mean = jnp.sum(out.reshape(surv, slot, block), axis=1) * (1.0 / pix)
                pooled[i * steps + step, :, span] = jnp.concatenate(
                    [mean, jnp.zeros((padded - surv, block), F32)], axis=0
                ).astype(BF16)
        if square:

            @pl.when(i + 3 < n_var)
            def _():
                pass_on(i + 3)

        return carry

    lax.fori_loop(0, n_var, variant, 0)

    count = n_var * steps * padded
    logits = lax.dot_general(
        pooled[...].reshape(count, width),
        readout[...],
        (((1,), (1,)), ((), ())),
        preferred_element_type=F32,
    )
    classes = logits.shape[1]
    top = jnp.max(logits, axis=1, keepdims=True)
    total = top + jnp.log(jnp.sum(jnp.exp(logits - top), axis=1, keepdims=True))
    wanted = jnp.concatenate(
        [labels[i // steps][:, 0:1] for i in range(n_var * steps)], axis=0
    )
    column = lax.broadcasted_iota(jnp.int32, (count, classes), 1)
    chosen = jnp.sum(jnp.where(column == wanted, logits, 0.0), axis=1, keepdims=True)
    kill = total - chosen
    row = lax.broadcasted_iota(jnp.int32, (count, 128), 0) % padded
    lane = lax.broadcasted_iota(jnp.int32, (count, 128), 1)
    spread = jnp.sum(
        jnp.where(row == lane, kill, 0.0).reshape(n_var * steps, padded, 128), axis=1
    )
    for i in range(n_var):
        kill_ref[i] = spread[i * steps : (i + 1) * steps, :surv]

    hand_over(1, 0).wait_send()
    for k in range(chips):
        for sign in (1, -1):

            @pl.when(reaches(-sign, k))
            def _():
                if k > 0:
                    hand_over(sign, k).wait_send()
                if k + 1 < chips:

                    @pl.when(reaches(sign, 1))
                    def _():
                        hop(sign, k).wait_send()


    def drain(i, carry):
        for which in range(2):
            for place in range(len(near)):
                own_copy(which, i, place).wait_send()
        if square:
            held_copy(0, i, 0, along).wait_send()
            held_copy(1, i, 1, across).wait_send()
        return carry

    lax.fori_loop(0, n_var, drain, 0)


def solution(mesh):
    n_mut, n_test = mesh.shape["mut"], mesh.shape["test"]

    def on_device(x, label, left, w1, w2, d1, d2, strength, readout):
        img_dev, pix, width = x.shape
        n_var, surv = left.shape
        steps = strength.shape[1]
        block, narrow = d1.shape[1], d1.shape[2]
        slot = round_up(pix, 16)
        padded = round_up(surv, 16)
        dma = pltpu.SemaphoreType.DMA
        places = max(3, n_test - 1)
        chips = n_mut // 2
        smem = pl.BlockSpec(memory_space=pltpu.SMEM)
        vmem = pl.BlockSpec(memory_space=pltpu.VMEM)
        anywhere = pl.BlockSpec(memory_space=pltpu.HBM)
        macs = n_var * steps * surv * slot * width * narrow * 2
        return pl.pallas_call(
            functools.partial(kernel, n_mut, n_test),
            out_shape=jax.ShapeDtypeStruct((n_var, steps, surv), F32),
            in_specs=[smem, smem, smem, vmem] + [anywhere] * 5,
            out_specs=vmem,
            scratch_shapes=[
                pltpu.VMEM((n_mut * img_dev, slot, width), BF16),
                pltpu.VMEM((n_var, n_test, block, narrow), BF16),
                pltpu.VMEM((n_var, n_test, narrow, block), BF16),
                pltpu.VMEM(w1.shape, BF16),
                pltpu.VMEM(w2.shape, BF16),
                pltpu.VMEM(readout.shape[::-1], BF16),
                pltpu.VMEM((surv * slot, width), BF16),
                pltpu.VMEM((width, narrow), BF16),
                pltpu.VMEM((n_var * steps, padded, width), BF16),
                pltpu.VMEM((n_var, padded, 128), jnp.int32),
                dma((5,)),
                dma((2, chips)),
                dma((2, chips)),
                dma((2, chips)),
                dma((2, chips)),
                dma((2, n_var, places)),
                dma((2, n_var, places)),
            ],
            compiler_params=pltpu.CompilerParams(
                collective_id=0, has_side_effects=True, vmem_limit_bytes=60 * 2**20
            ),
            cost_estimate=pl.CostEstimate(
                flops=2 * macs, bytes_accessed=8 * 2**20, transcendentals=0
            ),
        )(left, strength.T, label, x.transpose(1, 0, 2), d1, d2, w1, w2, readout.T)

    return jax.shard_map(
        on_device,
        mesh=mesh,
        in_specs=(
            P(("mut", "test"), None, None),
            P(),
            P("mut", "test"),
            P(),
            P(),
            P("mut", "test", None),
            P("mut", None, "test"),
            P("mut", None),
            P(),
        ),
        out_specs=P("mut", None, "test"),
        check_vma=False,
    )
```

```python
import functools

import jax
import jax.numpy as jnp
from jax import lax
from jax.experimental import pallas as pl
from jax.experimental.pallas import tpu as pltpu
from jax.sharding import PartitionSpec as P

MESH = pl.DeviceIdType.MESH
F32, BF16 = jnp.float32, jnp.bfloat16


def round_up(value, unit):
    return (value + unit - 1) // unit * unit


def kernel(
    n_mut,
    n_test,
    left_ref,
    left_rows,
    strength_ref,
    label_ref,
    x_ref,
    d1_ref,
    d2_ref,
    w1_ref,
    w2_ref,
    readout_ref,
    kill_ref,
    images,
    images2,
    d1_all,
    d2_all,
    w1,
    w2,
    readout,
    rows,
    w1_step,
    pooled,
    labels,
    local_sem,
    x_send,
    x_recv,
    sib_send,
    sib_recv,
    d_send,
    d_recv,
    cross_send,
    cross_recv,
    half_send,
    half_recv,
    sib2_send,
    sib2_recv,
    extra_send,
    extra_recv,
    table_out,
    table_in,
    table,
    scores_out,
    scores_in,
):
    pix, img_dev, width = x_ref.shape
    slot = images.shape[1]
    n_var, surv = left_ref.shape
    steps = strength_ref.shape[0]
    block = d1_ref.shape[1]
    narrow = d1_ref.shape[2]
    padded = pooled.shape[1]
    m, t = lax.axis_index("mut"), lax.axis_index("test")
    chips = n_mut // 2
    sibling = m + 1 - 2 * (m % 2)
    chip = m // 2
    square = n_test == 4 and n_var % 2 == 0
    mine = n_var // 2 if square else n_var
    shards = 2 if square else 1
    first = (t % 2) * mine if square else 0
    half = img_dev // 2
    if square:
        across, along = t + 1 - 2 * (t % 2), (t + 2) % 4
        near = [across, along]
        origin = [across, along, 3 - t]
    else:
        near = [(t + k) % n_test for k in range(1, n_test)]
        origin = [(t + n_test - k) % n_test for k in range(1, n_test)]

    def reaches(sign, k):
        return chip + k < chips if sign > 0 else chip >= k

    local = [
        pltpu.make_async_copy(w1_ref, w1, local_sem.at[0]),
        pltpu.make_async_copy(w2_ref, w2, local_sem.at[1]),
        pltpu.make_async_copy(readout_ref, readout, local_sem.at[2]),
        pltpu.make_async_copy(d1_ref.at[pl.ds(first, mine)], d1_all.at[:, t], local_sem.at[3]),
        pltpu.make_async_copy(d2_ref.at[pl.ds(first, mine)], d2_all.at[:, t], local_sem.at[4]),
    ]

    barrier = pltpu.get_barrier_semaphore()
    pl.semaphore_signal(barrier, inc=1, device_id=(sibling, t), device_id_type=MESH)
    for sign in (1, -1):

        @pl.when(reaches(sign, 1))
        def _():
            pl.semaphore_signal(
                barrier, inc=1, device_id=(m + 2 * sign, t), device_id_type=MESH
            )

    for peer in near:
        pl.semaphore_signal(barrier, inc=1, device_id=(m, peer), device_id_type=MESH)
    for copy in local:
        copy.start()
    for j in range(img_dev):
        images[m * img_dev + j] = jnp.concatenate(
            [x_ref[:, j, :], jnp.zeros((slot - pix, width), BF16)], axis=0
        )
    if square:
        table_out[...] = jnp.zeros_like(table_out)
        table_out[0:n_var, 0:surv] = left_rows[...]
    below = (chip + chips - 1) // chips
    above = (2 * chips - 2 - chip) // chips
    pl.semaphore_wait(barrier, 1 + len(near) + below + above)

    def x_copy(source, send, recv, target, shard=0, low=0, count=img_dev):
        held = images2 if shard else images
        view = held.at[pl.ds(source * img_dev + low, count)]
        return pltpu.make_async_remote_copy(
            view, view, send, recv, device_id=(target, t), device_id_type=MESH
        )

    def cross_copy(source, send, recv, low, count):
        return pltpu.make_async_remote_copy(
            images.at[pl.ds(source * img_dev + low, count)],
            images2.at[pl.ds(source * img_dev + low, count)],
            send,
            recv,
            device_id=(m, across),
            device_id_type=MESH,
        )

    def own_copy(which, i, place):
        ref, full = ((d1_ref, d1_all), (d2_ref, d2_all))[which]
        start = mine - first if square and place == 0 else first
        return pltpu.make_async_remote_copy(
            ref.at[start + i],
            full.at[i, t],
            d_send.at[which, i, place],
            d_recv.at[which, i, place],
            device_id=(m, near[place]),
            device_id_type=MESH,
        )

    def held_copy(which, i, place, target):
        view = (d1_all, d2_all)[which].at[i, origin[place]]
        return pltpu.make_async_remote_copy(
            view,
            view,
            d_send.at[which, i, 2],
            d_recv.at[which, i, 2],
            device_id=(m, target),
            device_id_type=MESH,
        )

    def arrived(which, i, place):
        view = (d1_all, d2_all)[which].at[i, origin[place]]
        pltpu.make_async_remote_copy(
            view,
            view,
            d_send.at[which, i, place],
            d_recv.at[which, i, place],
            device_id=(m, near[0]),
            device_id_type=MESH,
        ).wait_recv()

    def send_own(i):
        for which in range(2):
            for place in range(len(near)):
                own_copy(which, i, place).start()

    def pass_on(i):
        for which in range(2):
            arrived(which, i, 0)
            held_copy(which, i, 0, along).start()

    def hop(sign, k):
        way = (1 - sign) // 2
        return x_copy(
            m - 2 * sign * k, x_send.at[way, k], x_recv.at[way, k + 1], m + 2 * sign
        )

    def landed(sign, k):
        way = (1 - sign) // 2
        return x_copy(
            m - 2 * sign * k, x_send.at[way, k], x_recv.at[way, k], m + 2 * sign
        )

    def hand_over(sign, k):
        way = (1 - sign) // 2
        return x_copy(
            m - 2 * sign * k, sib_send.at[way, k], sib_recv.at[way, k], sibling
        )

    def handed(sign, k):
        way = (1 - sign) // 2
        return x_copy(
            sibling - 2 * sign * k, sib_send.at[way, k], sib_recv.at[way, k], sibling
        )

    def cross_back(sign, k):
        way = (1 - sign) // 2
        return cross_copy(
            m - 2 * sign * k,
            cross_send.at[way, k],
            cross_recv.at[way, k],
            half,
            img_dev - half,
        )

    def half_hop(sign, k):
        way = (1 - sign) // 2
        return x_copy(
            m - 2 * sign * k,
            half_send.at[way, k],
            half_recv.at[way, k + 1],
            m + 2 * sign,
            1,
            0,
            half,
        )

    def half_landed(sign, k):
        way = (1 - sign) // 2
        return x_copy(
            m - 2 * sign * k,
            half_send.at[way, k],
            half_recv.at[way, k],
            m + 2 * sign,
            1,
            0,
            half,
        )

    def second(origin_core, sign, k, piece):
        way = (1 - sign) // 2
        return x_copy(
            origin_core - 2 * sign * k,
            sib2_send.at[piece, way, k],
            sib2_recv.at[piece, way, k],
            sibling,
            1,
            piece * half,
            img_dev - half if piece else half,
        )

    def relay(k):
        for sign in (1, -1):

            @pl.when(reaches(-sign, k))
            def _():
                if k > 0:
                    landed(sign, k).wait_recv()
                if k + 1 < chips:

                    @pl.when(reaches(sign, 1))
                    def _():
                        hop(sign, k).start()

                if k > 0:
                    if square:
                        cross_back(sign, k).start()
                    hand_over(sign, k).start()

    def relay_half(k):
        for sign in (1, -1):

            @pl.when(reaches(-sign, k))
            def _():
                if k > 0:
                    half_landed(sign, k).wait_recv()
                if k + 1 < chips:

                    @pl.when(reaches(sign, 1))
                    def _():
                        half_hop(sign, k).start()

                if k > 0:
                    second(m, sign, k, 0).start()

    def share_cross(k):
        for sign in (1, -1):

            @pl.when(reaches(-sign, k))
            def _():
                cross_back(sign, k).wait_recv()
                second(m, sign, k, 1).start()

    def own_cross():
        return cross_copy(m, extra_send.at[0], extra_recv.at[0], 0, img_dev)

    def own_second(core):
        return x_copy(core, extra_send.at[1], extra_recv.at[1], sibling, 1)

    def send_table():
        return pltpu.make_async_remote_copy(
            table_out,
            table_in,
            extra_send.at[2],
            extra_recv.at[2],
            device_id=(m, across),
            device_id_type=MESH,
        )

    def send_scores():
        return pltpu.make_async_remote_copy(
            scores_out,
            scores_in,
            extra_send.at[3],
            extra_recv.at[3],
            device_id=(m, across),
            device_id_type=MESH,
        )

    relay(0)
    hand_over(1, 0).start()
    for i in range(mine):
        send_own(i)
    if square:
        own_cross().start()
        send_table().start()
        for k in range(1, chips):
            if k - 1 < mine:
                pass_on(k - 1)
            if k == chips - 1:
                own_cross().wait_recv()
                relay_half(0)
                own_second(m).start()
            relay(k)
        for i in range(max(chips - 1, 0), mine):
            pass_on(i)
        send_table().wait_recv()
        read_table = pltpu.make_async_copy(table_in, table, local_sem.at[5])
        read_table.start()
        read_table.wait()
        relay_half(1)
    else:
        for k in range(1, chips):
            relay(k)
    handed(1, 0).wait_recv()
    for k in range(1, chips):
        for sign in (1, -1):

            @pl.when(reaches(-sign, k))
            def _():
                handed(sign, k).wait_recv()

    def rest(early):
        if early:
            relay_half(2)
            share_cross(1)
            return
        for k in range(3, chips):
            relay_half(k)
        for k in range(2, chips):
            share_cross(k)
        own_second(sibling).wait_recv()
        for k in range(1, chips):
            for sign in (1, -1):

                @pl.when(reaches(-sign, k))
                def _():
                    for piece in range(2):
                        second(sibling, sign, k, piece).wait_recv()

    for copy in local:
        copy.wait()

    def variant(q, carry):
        i = q % mine
        if square:

            @pl.when(q == 1)
            def _():
                rest(True)

            @pl.when(q == mine)
            def _():
                rest(False)

        @pl.when(q < mine)
        def _():
            for which in range(2):
                for place in range(1 if square else 0, len(origin)):
                    arrived(which, i, place)

        def gather(held, entries, test):
            for j in range(surv):
                entry = entries[first + i, j]
                rows[pl.ds(j * slot, slot), :] = held[entry]
                number = (entry // img_dev * n_test + test) * img_dev + entry % img_dev
                labels[q, pl.ds(j, 1), :] = jnp.full(
                    (1, 128), label_ref[number], jnp.int32
                )

        @pl.when(q < mine)
        def _():
            gather(images, left_ref, t)

        if square:

            @pl.when(q >= mine)
            def _():
                gather(images2, table, across)

        for step in range(steps):
            strength = strength_ref[step, first + i]
            for part in range(n_test):
                span = pl.ds(part * block, block)
                w1_step[span, :] = (
                    w1[span, :].astype(F32) + strength * d1_all[i, part].astype(F32)
                ).astype(BF16)
            hidden = jnp.maximum(
                jnp.dot(rows[...], w1_step[...], preferred_element_type=F32), 0.0
            ).astype(BF16)
            for part in range(n_test):
                span = pl.ds(part * block, block)
                w2_step = (
                    w2[:, span].astype(F32) + strength * d2_all[i, part].astype(F32)
                ).astype(BF16)
                out = jnp.maximum(
                    jnp.dot(hidden, w2_step, preferred_element_type=F32)
                    + rows[:, span].astype(F32),
                    0.0,
                )
                mean = jnp.sum(out.reshape(surv, slot, block), axis=1) * (1.0 / pix)
                pooled[q * steps + step, :, span] = jnp.concatenate(
                    [mean, jnp.zeros((padded - surv, block), F32)], axis=0
                ).astype(BF16)
        return carry

    groups = mine * shards
    lax.fori_loop(0, groups, variant, 0)

    count = groups * steps * padded
    logits = lax.dot_general(
        pooled[...].reshape(count, width),
        readout[...],
        (((1,), (1,)), ((), ())),
        preferred_element_type=F32,
    )
    classes = logits.shape[1]
    top = jnp.max(logits, axis=1, keepdims=True)
    total = top + jnp.log(jnp.sum(jnp.exp(logits - top), axis=1, keepdims=True))
    wanted = jnp.concatenate(
        [labels[i // steps][:, 0:1] for i in range(groups * steps)], axis=0
    )
    column = lax.broadcasted_iota(jnp.int32, (count, classes), 1)
    chosen = jnp.sum(jnp.where(column == wanted, logits, 0.0), axis=1, keepdims=True)
    kill = total - chosen
    row = lax.broadcasted_iota(jnp.int32, (count, 128), 0) % padded
    lane = lax.broadcasted_iota(jnp.int32, (count, 128), 1)
    spread = jnp.sum(
        jnp.where(row == lane, kill, 0.0).reshape(groups * steps, padded, 128), axis=1
    )
    if square:
        scores_out[...] = spread
        send_scores().start()
    for i in range(mine):
        kill_ref[first + i] = spread[i * steps : (i + 1) * steps, :surv]
    if square:
        send_scores().wait_recv()
        for i in range(mine):
            low = (mine + i) * steps
            kill_ref[mine - first + i] = scores_in[low : low + steps, :surv]

    hand_over(1, 0).wait_send()
    for k in range(chips):
        for sign in (1, -1):

            @pl.when(reaches(-sign, k))
            def _():
                if k > 0:
                    hand_over(sign, k).wait_send()
                if k + 1 < chips:

                    @pl.when(reaches(sign, 1))
                    def _():
                        hop(sign, k).wait_send()


    def drain(i, carry):
        for which in range(2):
            for place in range(len(near)):
                own_copy(which, i, place).wait_send()
            if square:
                held_copy(which, i, 0, along).wait_send()
        return carry

    lax.fori_loop(0, mine, drain, 0)
    if square:
        own_cross().wait_send()
        own_second(m).wait_send()
        send_table().wait_send()
        send_scores().wait_send()
        for k in range(chips):
            for sign in (1, -1):

                @pl.when(reaches(-sign, k))
                def _():
                    if k > 0:
                        cross_back(sign, k).wait_send()
                        second(m, sign, k, 0).wait_send()
                        second(m, sign, k, 1).wait_send()
                    if k + 1 < chips:

                        @pl.when(reaches(sign, 1))
                        def _():
                            half_hop(sign, k).wait_send()


def solution(mesh):
    n_mut, n_test = mesh.shape["mut"], mesh.shape["test"]

    def on_device(x, label, left, w1, w2, d1, d2, strength, readout):
        img_dev, pix, width = x.shape
        n_var, surv = left.shape
        steps = strength.shape[1]
        block, narrow = d1.shape[1], d1.shape[2]
        slot = round_up(pix, 16)
        padded = round_up(surv, 16)
        dma = pltpu.SemaphoreType.DMA
        places = max(3, n_test - 1)
        square = n_test == 4 and n_var % 2 == 0
        mine = n_var // 2 if square else n_var
        groups = n_var
        chips = n_mut // 2
        smem = pl.BlockSpec(memory_space=pltpu.SMEM)
        vmem = pl.BlockSpec(memory_space=pltpu.VMEM)
        anywhere = pl.BlockSpec(memory_space=pltpu.HBM)
        macs = n_var * steps * surv * slot * width * narrow * 2
        return pl.pallas_call(
            functools.partial(kernel, n_mut, n_test),
            out_shape=jax.ShapeDtypeStruct((n_var, steps, surv), F32),
            in_specs=[smem, vmem, smem, smem, vmem] + [anywhere] * 5,
            out_specs=vmem,
            scratch_shapes=[
                pltpu.VMEM((n_mut * img_dev, slot, width), BF16),
                pltpu.VMEM((n_mut * img_dev, slot, width), BF16),
                pltpu.VMEM((mine, n_test, block, narrow), BF16),
                pltpu.VMEM((mine, n_test, narrow, block), BF16),
                pltpu.VMEM(w1.shape, BF16),
                pltpu.VMEM(w2.shape, BF16),
                pltpu.VMEM(readout.shape[::-1], BF16),
                pltpu.VMEM((surv * slot, width), BF16),
                pltpu.VMEM((width, narrow), BF16),
                pltpu.VMEM((groups * steps, padded, width), BF16),
                pltpu.VMEM((groups, padded, 128), jnp.int32),
                dma((6,)),
                dma((2, chips)),
                dma((2, chips)),
                dma((2, chips)),
                dma((2, chips)),
                dma((2, n_var, places)),
                dma((2, n_var, places)),
                dma((2, chips)),
                dma((2, chips)),
                dma((2, chips)),
                dma((2, chips)),
                dma((2, 2, chips)),
                dma((2, 2, chips)),
                dma((4,)),
                dma((4,)),
                pltpu.VMEM((round_up(n_var, 8), 128), jnp.int32),
                pltpu.VMEM((round_up(n_var, 8), 128), jnp.int32),
                pltpu.SMEM((round_up(n_var, 8), 128), jnp.int32),
                pltpu.VMEM((groups * steps, 128), F32),
                pltpu.VMEM((groups * steps, 128), F32),
            ],
            compiler_params=pltpu.CompilerParams(
                collective_id=0, has_side_effects=True, vmem_limit_bytes=60 * 2**20
            ),
            cost_estimate=pl.CostEstimate(
                flops=2 * macs, bytes_accessed=8 * 2**20, transcendentals=0
            ),
        )(left, left, strength.T, label, x.transpose(1, 0, 2), d1, d2, w1, w2, readout.T)

    return jax.shard_map(
        on_device,
        mesh=mesh,
        in_specs=(
            P(("mut", "test"), None, None),
            P(),
            P("mut", "test"),
            P(),
            P(),
            P("mut", "test", None),
            P("mut", None, "test"),
            P("mut", None),
            P(),
        ),
        out_specs=P("mut", None, "test"),
        check_vma=False,
    )
```

```python
import functools

import jax
import jax.numpy as jnp
from jax import lax
from jax.experimental import pallas as pl
from jax.experimental.pallas import tpu as pltpu
from jax.sharding import PartitionSpec as P

MESH = pl.DeviceIdType.MESH
F32, BF16 = jnp.float32, jnp.bfloat16


def round_up(value, unit):
    return (value + unit - 1) // unit * unit


def kernel(
    n_mut,
    n_test,
    left_ref,
    left_rows,
    strength_ref,
    label_ref,
    x_ref,
    d1_ref,
    d2_ref,
    w1_ref,
    w2_ref,
    readout_ref,
    kill_ref,
    images,
    images2,
    d1_all,
    d2_all,
    w1,
    w2,
    readout,
    rows,
    w1_step,
    w2_step,
    pooled,
    labels,
    local_sem,
    x_send,
    x_recv,
    sib_send,
    sib_recv,
    d_send,
    d_recv,
    cross_send,
    cross_recv,
    half_send,
    half_recv,
    sib2_send,
    sib2_recv,
    extra_send,
    extra_recv,
    table_out,
    table_in,
    table,
    scores_out,
    scores_in,
):
    pix, img_dev, width = x_ref.shape
    slot = images.shape[1]
    n_var, surv = left_ref.shape
    steps = strength_ref.shape[0]
    block = d1_ref.shape[1]
    narrow = d1_ref.shape[2]
    padded = pooled.shape[1]
    m, t = lax.axis_index("mut"), lax.axis_index("test")
    chips = n_mut // 2
    sibling = m + 1 - 2 * (m % 2)
    chip = m // 2
    square = n_test == 4 and n_var % 2 == 0
    mine = n_var // 2 if square else n_var
    shards = 2 if square else 1
    first = (t % 2) * mine if square else 0
    half = img_dev // 2
    if square:
        across, along = t + 1 - 2 * (t % 2), (t + 2) % 4
        near = [across, along]
        origin = [across, along, 3 - t]
    else:
        near = [(t + k) % n_test for k in range(1, n_test)]
        origin = [(t + n_test - k) % n_test for k in range(1, n_test)]

    def reaches(sign, k):
        return chip + k < chips if sign > 0 else chip >= k

    local = [
        pltpu.make_async_copy(w1_ref, w1, local_sem.at[0]),
        pltpu.make_async_copy(w2_ref, w2, local_sem.at[1]),
        pltpu.make_async_copy(readout_ref, readout, local_sem.at[2]),
        pltpu.make_async_copy(d1_ref.at[pl.ds(first, mine)], d1_all.at[:, t], local_sem.at[3]),
        pltpu.make_async_copy(d2_ref.at[pl.ds(first, mine)], d2_all.at[:, t], local_sem.at[4]),
    ]

    barrier = pltpu.get_barrier_semaphore()
    pl.semaphore_signal(barrier, inc=1, device_id=(sibling, t), device_id_type=MESH)
    for sign in (1, -1):

        @pl.when(reaches(sign, 1))
        def _():
            pl.semaphore_signal(
                barrier, inc=1, device_id=(m + 2 * sign, t), device_id_type=MESH
            )

    for peer in near:
        pl.semaphore_signal(barrier, inc=1, device_id=(m, peer), device_id_type=MESH)
    for copy in local:
        copy.start()
    for j in range(img_dev):
        images[m * img_dev + j] = jnp.concatenate(
            [x_ref[:, j, :], jnp.zeros((slot - pix, width), BF16)], axis=0
        )
    if square:
        table_out[...] = jnp.zeros_like(table_out)
        table_out[0:n_var, 0:surv] = left_rows[...]
    below = (chip + chips - 1) // chips
    above = (2 * chips - 2 - chip) // chips
    pl.semaphore_wait(barrier, 1 + len(near) + below + above)

    def x_copy(source, send, recv, target, shard=0, low=0, count=img_dev):
        held = images2 if shard else images
        view = held.at[pl.ds(source * img_dev + low, count)]
        return pltpu.make_async_remote_copy(
            view, view, send, recv, device_id=(target, t), device_id_type=MESH
        )

    def cross_copy(source, send, recv, low, count):
        return pltpu.make_async_remote_copy(
            images.at[pl.ds(source * img_dev + low, count)],
            images2.at[pl.ds(source * img_dev + low, count)],
            send,
            recv,
            device_id=(m, across),
            device_id_type=MESH,
        )

    def own_copy(which, i, place):
        ref, full = ((d1_ref, d1_all), (d2_ref, d2_all))[which]
        start = mine - first if square and place == 0 else first
        return pltpu.make_async_remote_copy(
            ref.at[start + i],
            full.at[i, t],
            d_send.at[which, i, place],
            d_recv.at[which, i, place],
            device_id=(m, near[place]),
            device_id_type=MESH,
        )

    def held_copy(which, i, place, target):
        view = (d1_all, d2_all)[which].at[i, origin[place]]
        return pltpu.make_async_remote_copy(
            view,
            view,
            d_send.at[which, i, 2],
            d_recv.at[which, i, 2],
            device_id=(m, target),
            device_id_type=MESH,
        )

    def arrived(which, i, place):
        view = (d1_all, d2_all)[which].at[i, origin[place]]
        pltpu.make_async_remote_copy(
            view,
            view,
            d_send.at[which, i, place],
            d_recv.at[which, i, place],
            device_id=(m, near[0]),
            device_id_type=MESH,
        ).wait_recv()

    def send_own(i):
        for which in range(2):
            for place in range(len(near)):
                own_copy(which, i, place).start()

    def pass_on(i):
        for which in range(2):
            arrived(which, i, 0)
            held_copy(which, i, 0, along).start()

    def hop(sign, k):
        way = (1 - sign) // 2
        return x_copy(
            m - 2 * sign * k, x_send.at[way, k], x_recv.at[way, k + 1], m + 2 * sign
        )

    def landed(sign, k):
        way = (1 - sign) // 2
        return x_copy(
            m - 2 * sign * k, x_send.at[way, k], x_recv.at[way, k], m + 2 * sign
        )

    def hand_over(sign, k):
        way = (1 - sign) // 2
        return x_copy(
            m - 2 * sign * k, sib_send.at[way, k], sib_recv.at[way, k], sibling
        )

    def handed(sign, k):
        way = (1 - sign) // 2
        return x_copy(
            sibling - 2 * sign * k, sib_send.at[way, k], sib_recv.at[way, k], sibling
        )

    def cross_back(sign, k):
        way = (1 - sign) // 2
        return cross_copy(
            m - 2 * sign * k,
            cross_send.at[way, k],
            cross_recv.at[way, k],
            half,
            img_dev - half,
        )

    def half_hop(sign, k):
        way = (1 - sign) // 2
        return x_copy(
            m - 2 * sign * k,
            half_send.at[way, k],
            half_recv.at[way, k + 1],
            m + 2 * sign,
            1,
            0,
            half,
        )

    def half_landed(sign, k):
        way = (1 - sign) // 2
        return x_copy(
            m - 2 * sign * k,
            half_send.at[way, k],
            half_recv.at[way, k],
            m + 2 * sign,
            1,
            0,
            half,
        )

    def second(origin_core, sign, k, piece):
        way = (1 - sign) // 2
        return x_copy(
            origin_core - 2 * sign * k,
            sib2_send.at[piece, way, k],
            sib2_recv.at[piece, way, k],
            sibling,
            1,
            piece * half,
            img_dev - half if piece else half,
        )

    def relay(k):
        for sign in (1, -1):

            @pl.when(reaches(-sign, k))
            def _():
                if k > 0:
                    landed(sign, k).wait_recv()
                if k + 1 < chips:

                    @pl.when(reaches(sign, 1))
                    def _():
                        hop(sign, k).start()

                if k > 0:
                    if square:
                        cross_back(sign, k).start()
                    hand_over(sign, k).start()

    def relay_half(k):
        for sign in (1, -1):

            @pl.when(reaches(-sign, k))
            def _():
                if k > 0:
                    half_landed(sign, k).wait_recv()
                if k + 1 < chips:

                    @pl.when(reaches(sign, 1))
                    def _():
                        half_hop(sign, k).start()

                if k > 0:
                    second(m, sign, k, 0).start()

    def share_cross(k):
        for sign in (1, -1):

            @pl.when(reaches(-sign, k))
            def _():
                cross_back(sign, k).wait_recv()
                second(m, sign, k, 1).start()

    def own_cross():
        return cross_copy(m, extra_send.at[0], extra_recv.at[0], 0, img_dev)

    def own_second(core):
        return x_copy(core, extra_send.at[1], extra_recv.at[1], sibling, 1)

    def send_table():
        return pltpu.make_async_remote_copy(
            table_out,
            table_in,
            extra_send.at[2],
            extra_recv.at[2],
            device_id=(m, across),
            device_id_type=MESH,
        )

    def send_scores():
        return pltpu.make_async_remote_copy(
            scores_out,
            scores_in,
            extra_send.at[3],
            extra_recv.at[3],
            device_id=(m, across),
            device_id_type=MESH,
        )

    relay(0)
    hand_over(1, 0).start()
    for i in range(mine):
        send_own(i)
    if square:
        own_cross().start()
        send_table().start()
        for k in range(1, chips):
            if k - 1 < mine:
                pass_on(k - 1)
            if k == chips - 1:
                own_cross().wait_recv()
                relay_half(0)
                own_second(m).start()
            relay(k)
        for i in range(max(chips - 1, 0), mine):
            pass_on(i)
        send_table().wait_recv()
        read_table = pltpu.make_async_copy(table_in, table, local_sem.at[5])
        read_table.start()
        read_table.wait()
        relay_half(1)
    else:
        for k in range(1, chips):
            relay(k)
    def rest(early):
        if early:
            relay_half(2)
            share_cross(1)
            return
        for k in range(3, chips):
            relay_half(k)
        for k in range(2, chips):
            share_cross(k)
        keep_own()
        own_second(sibling).wait_recv()
        for k in range(1, chips):
            for sign in (1, -1):

                @pl.when(reaches(-sign, k))
                def _():
                    for piece in range(2):
                        second(sibling, sign, k, piece).wait_recv()

    def finish(base, number):
        count = number * padded
        logits = lax.dot_general(
            pooled[base : base + number].reshape(count, width),
            readout[...],
            (((1,), (1,)), ((), ())),
            preferred_element_type=F32,
        )
        classes = logits.shape[1]
        top = jnp.max(logits, axis=1, keepdims=True)
        total = top + jnp.log(jnp.sum(jnp.exp(logits - top), axis=1, keepdims=True))
        wanted = jnp.concatenate(
            [labels[i // steps][:, 0:1] for i in range(base, base + number)], axis=0
        )
        column = lax.broadcasted_iota(jnp.int32, (count, classes), 1)
        chosen = jnp.sum(jnp.where(column == wanted, logits, 0.0), axis=1, keepdims=True)
        kill = total - chosen
        row = lax.broadcasted_iota(jnp.int32, (count, 128), 0) % padded
        lane = lax.broadcasted_iota(jnp.int32, (count, 128), 1)
        return jnp.sum(
            jnp.where(row == lane, kill, 0.0).reshape(number, padded, 128), axis=1
        )

    def keep_own():
        spread = finish(0, mine * steps)
        for i in range(mine):
            kill_ref[first + i] = spread[i * steps : (i + 1) * steps, :surv]

    def build(i):
        for which in range(2):
            for place in range(1 if square else 0, len(origin)):
                arrived(which, i, place)
        for part in range(n_test):
            span = pl.ds(part * block, block)
            base1, delta1 = w1[span, :].astype(F32), d1_all[i, part].astype(F32)
            base2, delta2 = w2[:, span].astype(F32), d2_all[i, part].astype(F32)
            for step in range(steps):
                strength = strength_ref[step, first + i]
                w1_step[i, span, pl.ds(step * narrow, narrow)] = (
                    base1 + strength * delta1
                ).astype(BF16)
                w2_step[i, step, :, span] = (base2 + strength * delta2).astype(BF16)

    def variant(q, carry):
        i = q % mine
        if square:

            @pl.when(q == 1)
            def _():
                rest(True)

            @pl.when(q == mine)
            def _():
                rest(False)

        @pl.when((q > 0) & (q < mine))
        def _():
            build(i)

        def gather(held, entries, test):
            for j in range(surv):
                entry = entries[first + i, j]
                rows[pl.ds(j * slot, slot), :] = held[entry]
                number = (entry // img_dev * n_test + test) * img_dev + entry % img_dev
                labels[q, pl.ds(j, 1), :] = jnp.full(
                    (1, 128), label_ref[number], jnp.int32
                )

        @pl.when(q < mine)
        def _():
            gather(images, left_ref, t)

        if square:

            @pl.when(q >= mine)
            def _():
                gather(images2, table, across)

        hidden = jnp.maximum(
            jnp.dot(rows[...], w1_step[i], preferred_element_type=F32), 0.0
        ).astype(BF16)
        for low in range(0, width, narrow):
            span = pl.ds(low, narrow)
            residual = rows[:, span].astype(F32)
            for step in range(steps):
                out = jnp.maximum(
                    jnp.dot(
                        hidden[:, step * narrow : (step + 1) * narrow],
                        w2_step[i, step, :, span],
                        preferred_element_type=F32,
                    )
                    + residual,
                    0.0,
                )
                mean = jnp.sum(out.reshape(surv, slot, narrow), axis=1) * (1.0 / pix)
                pooled[q * steps + step, :, span] = jnp.concatenate(
                    [mean, jnp.zeros((padded - surv, narrow), F32)], axis=0
                ).astype(BF16)
        return carry

    for copy in local:
        copy.wait()
    build(0)
    handed(1, 0).wait_recv()
    for k in range(1, chips):
        for sign in (1, -1):

            @pl.when(reaches(-sign, k))
            def _():
                handed(sign, k).wait_recv()

    groups = mine * shards
    lax.fori_loop(0, groups, variant, 0)

    if square:
        scores_out[...] = finish(mine * steps, mine * steps)
        send_scores().start()
        send_scores().wait_recv()
        for i in range(mine):
            kill_ref[mine - first + i] = scores_in[i * steps : (i + 1) * steps, :surv]
    else:
        keep_own()

    hand_over(1, 0).wait_send()
    for k in range(chips):
        for sign in (1, -1):

            @pl.when(reaches(-sign, k))
            def _():
                if k > 0:
                    hand_over(sign, k).wait_send()
                if k + 1 < chips:

                    @pl.when(reaches(sign, 1))
                    def _():
                        hop(sign, k).wait_send()


    def drain(i, carry):
        for which in range(2):
            for place in range(len(near)):
                own_copy(which, i, place).wait_send()
            if square:
                held_copy(which, i, 0, along).wait_send()
        return carry

    lax.fori_loop(0, mine, drain, 0)
    if square:
        own_cross().wait_send()
        own_second(m).wait_send()
        send_table().wait_send()
        send_scores().wait_send()
        for k in range(chips):
            for sign in (1, -1):

                @pl.when(reaches(-sign, k))
                def _():
                    if k > 0:
                        cross_back(sign, k).wait_send()
                        second(m, sign, k, 0).wait_send()
                        second(m, sign, k, 1).wait_send()
                    if k + 1 < chips:

                        @pl.when(reaches(sign, 1))
                        def _():
                            half_hop(sign, k).wait_send()


def solution(mesh):
    n_mut, n_test = mesh.shape["mut"], mesh.shape["test"]

    def on_device(x, label, left, w1, w2, d1, d2, strength, readout):
        img_dev, pix, width = x.shape
        n_var, surv = left.shape
        steps = strength.shape[1]
        block, narrow = d1.shape[1], d1.shape[2]
        slot = round_up(pix, 16)
        padded = round_up(surv, 16)
        dma = pltpu.SemaphoreType.DMA
        places = max(3, n_test - 1)
        square = n_test == 4 and n_var % 2 == 0
        mine = n_var // 2 if square else n_var
        groups = n_var
        chips = n_mut // 2
        smem = pl.BlockSpec(memory_space=pltpu.SMEM)
        vmem = pl.BlockSpec(memory_space=pltpu.VMEM)
        anywhere = pl.BlockSpec(memory_space=pltpu.HBM)
        macs = n_var * steps * surv * slot * width * narrow * 2
        return pl.pallas_call(
            functools.partial(kernel, n_mut, n_test),
            out_shape=jax.ShapeDtypeStruct((n_var, steps, surv), F32),
            in_specs=[smem, vmem, smem, smem, vmem] + [anywhere] * 5,
            out_specs=vmem,
            scratch_shapes=[
                pltpu.VMEM((n_mut * img_dev, slot, width), BF16),
                pltpu.VMEM((n_mut * img_dev, slot, width), BF16),
                pltpu.VMEM((mine, n_test, block, narrow), BF16),
                pltpu.VMEM((mine, n_test, narrow, block), BF16),
                pltpu.VMEM(w1.shape, BF16),
                pltpu.VMEM(w2.shape, BF16),
                pltpu.VMEM(readout.shape[::-1], BF16),
                pltpu.VMEM((surv * slot, width), BF16),
                pltpu.VMEM((mine, width, steps * narrow), BF16),
                pltpu.VMEM((mine, steps, narrow, width), BF16),
                pltpu.VMEM((groups * steps, padded, width), BF16),
                pltpu.VMEM((groups, padded, 128), jnp.int32),
                dma((6,)),
                dma((2, chips)),
                dma((2, chips)),
                dma((2, chips)),
                dma((2, chips)),
                dma((2, n_var, places)),
                dma((2, n_var, places)),
                dma((2, chips)),
                dma((2, chips)),
                dma((2, chips)),
                dma((2, chips)),
                dma((2, 2, chips)),
                dma((2, 2, chips)),
                dma((4,)),
                dma((4,)),
                pltpu.VMEM((round_up(n_var, 8), 128), jnp.int32),
                pltpu.VMEM((round_up(n_var, 8), 128), jnp.int32),
                pltpu.SMEM((round_up(n_var, 8), 128), jnp.int32),
                pltpu.VMEM((mine * steps, 128), F32),
                pltpu.VMEM((mine * steps, 128), F32),
            ],
            compiler_params=pltpu.CompilerParams(
                collective_id=0, has_side_effects=True, vmem_limit_bytes=60 * 2**20
            ),
            cost_estimate=pl.CostEstimate(
                flops=2 * macs, bytes_accessed=8 * 2**20, transcendentals=0
            ),
        )(left, left, strength.T, label, x.transpose(1, 0, 2), d1, d2, w1, w2, readout.T)

    return jax.shard_map(
        on_device,
        mesh=mesh,
        in_specs=(
            P(("mut", "test"), None, None),
            P(),
            P("mut", "test"),
            P(),
            P(),
            P("mut", "test", None),
            P("mut", None, "test"),
            P("mut", None),
            P(),
        ),
        out_specs=P("mut", None, "test"),
        check_vma=False,
    )
```

```python
import functools

import jax
import jax.numpy as jnp
from jax import lax
from jax.experimental import pallas as pl
from jax.experimental.pallas import tpu as pltpu
from jax.sharding import PartitionSpec as P

MESH = pl.DeviceIdType.MESH
F32, BF16 = jnp.float32, jnp.bfloat16


def round_up(value, unit):
    return (value + unit - 1) // unit * unit


def kernel(
    n_mut,
    n_test,
    left_ref,
    left_rows,
    strength_ref,
    label_ref,
    x_ref,
    d1_ref,
    d2_ref,
    w1_ref,
    w2_ref,
    readout_ref,
    kill_ref,
    images,
    images2,
    d1_all,
    d2_all,
    w1,
    w2,
    readout,
    rows,
    w1_step,
    w2_step,
    pooled,
    labels,
    local_sem,
    x_send,
    x_recv,
    sib_send,
    sib_recv,
    d_send,
    d_recv,
    cross_send,
    cross_recv,
    half_send,
    half_recv,
    sib2_send,
    sib2_recv,
    extra_send,
    extra_recv,
    table_out,
    table_in,
    table,
    scores_out,
    scores_in,
):
    pix, img_dev, width = x_ref.shape
    slot = images.shape[1]
    n_var, surv = left_ref.shape
    steps = strength_ref.shape[0]
    block = d1_ref.shape[1]
    narrow = d1_ref.shape[2]
    padded = pooled.shape[1]
    m, t = lax.axis_index("mut"), lax.axis_index("test")
    chips = n_mut // 2
    sibling = m + 1 - 2 * (m % 2)
    chip = m // 2
    square = n_test == 4 and n_var == 4 and chips == 4
    mine = n_var // 2 if square else n_var
    shards = 2 if square else 1
    first = (t % 2) * mine if square else 0
    half = img_dev // 2
    if square:
        across, along = t + 1 - 2 * (t % 2), (t + 2) % 4
        near = [across, along]
        origin = [across, along, 3 - t]
    else:
        near = [(t + k) % n_test for k in range(1, n_test)]
        origin = [(t + n_test - k) % n_test for k in range(1, n_test)]

    def reaches(sign, k):
        return chip + k < chips if sign > 0 else chip >= k

    local = [
        pltpu.make_async_copy(w1_ref, w1, local_sem.at[0]),
        pltpu.make_async_copy(w2_ref, w2, local_sem.at[1]),
        pltpu.make_async_copy(readout_ref, readout, local_sem.at[2]),
        pltpu.make_async_copy(d1_ref.at[pl.ds(first, mine)], d1_all.at[:, t], local_sem.at[3]),
        pltpu.make_async_copy(d2_ref.at[pl.ds(first, mine)], d2_all.at[:, t], local_sem.at[4]),
    ]

    barrier = pltpu.get_barrier_semaphore()
    pl.semaphore_signal(barrier, inc=1, device_id=(sibling, t), device_id_type=MESH)
    for sign in (1, -1):

        @pl.when(reaches(sign, 1))
        def _():
            pl.semaphore_signal(
                barrier, inc=1, device_id=(m + 2 * sign, t), device_id_type=MESH
            )

    for peer in near:
        pl.semaphore_signal(barrier, inc=1, device_id=(m, peer), device_id_type=MESH)
    for copy in local:
        copy.start()
    for j in range(img_dev):
        images[m * img_dev + j] = jnp.concatenate(
            [x_ref[:, j, :], jnp.zeros((slot - pix, width), BF16)], axis=0
        )
    if square:
        table_out[...] = jnp.zeros_like(table_out)
        table_out[0:n_var, 0:surv] = left_rows[...]
    below = (chip + chips - 1) // chips
    above = (2 * chips - 2 - chip) // chips
    pl.semaphore_wait(barrier, 1 + len(near) + below + above)

    def x_copy(source, send, recv, target, shard=0, low=0, count=img_dev):
        held = images2 if shard else images
        view = held.at[pl.ds(source * img_dev + low, count)]
        return pltpu.make_async_remote_copy(
            view, view, send, recv, device_id=(target, t), device_id_type=MESH
        )

    def cross_copy(source, send, recv, low, count):
        return pltpu.make_async_remote_copy(
            images.at[pl.ds(source * img_dev + low, count)],
            images2.at[pl.ds(source * img_dev + low, count)],
            send,
            recv,
            device_id=(m, across),
            device_id_type=MESH,
        )

    def own_copy(which, i, place):
        ref, full = ((d1_ref, d1_all), (d2_ref, d2_all))[which]
        start = mine - first if square and place == 0 else first
        return pltpu.make_async_remote_copy(
            ref.at[start + i],
            full.at[i, t],
            d_send.at[which, i, place],
            d_recv.at[which, i, place],
            device_id=(m, near[place]),
            device_id_type=MESH,
        )

    def held_copy(which, i, place, target):
        view = (d1_all, d2_all)[which].at[i, origin[place]]
        return pltpu.make_async_remote_copy(
            view,
            view,
            d_send.at[which, i, 2],
            d_recv.at[which, i, 2],
            device_id=(m, target),
            device_id_type=MESH,
        )

    def arrived(which, i, place):
        view = (d1_all, d2_all)[which].at[i, origin[place]]
        pltpu.make_async_remote_copy(
            view,
            view,
            d_send.at[which, i, place],
            d_recv.at[which, i, place],
            device_id=(m, near[0]),
            device_id_type=MESH,
        ).wait_recv()

    def send_own(i):
        for which in range(2):
            for place in range(len(near)):
                own_copy(which, i, place).start()

    def pass_on(i):
        for which in range(2):
            arrived(which, i, 0)
            held_copy(which, i, 0, along).start()

    def hop(sign, k):
        way = (1 - sign) // 2
        return x_copy(
            m - 2 * sign * k, x_send.at[way, k], x_recv.at[way, k + 1], m + 2 * sign
        )

    def landed(sign, k):
        way = (1 - sign) // 2
        return x_copy(
            m - 2 * sign * k, x_send.at[way, k], x_recv.at[way, k], m + 2 * sign
        )

    def hand_over(sign, k):
        way = (1 - sign) // 2
        return x_copy(
            m - 2 * sign * k, sib_send.at[way, k], sib_recv.at[way, k], sibling
        )

    def handed(sign, k):
        way = (1 - sign) // 2
        return x_copy(
            sibling - 2 * sign * k, sib_send.at[way, k], sib_recv.at[way, k], sibling
        )

    def cross_back(sign, k):
        way = (1 - sign) // 2
        return cross_copy(
            m - 2 * sign * k,
            cross_send.at[way, k],
            cross_recv.at[way, k],
            half,
            img_dev - half,
        )

    def half_hop(sign, k):
        way = (1 - sign) // 2
        return x_copy(
            m - 2 * sign * k,
            half_send.at[way, k],
            half_recv.at[way, k + 1],
            m + 2 * sign,
            1,
            0,
            half,
        )

    def half_landed(sign, k):
        way = (1 - sign) // 2
        return x_copy(
            m - 2 * sign * k,
            half_send.at[way, k],
            half_recv.at[way, k],
            m + 2 * sign,
            1,
            0,
            half,
        )

    def second(origin_core, sign, k, piece):
        way = (1 - sign) // 2
        return x_copy(
            origin_core - 2 * sign * k,
            sib2_send.at[piece, way, k],
            sib2_recv.at[piece, way, k],
            sibling,
            1,
            piece * half,
            img_dev - half if piece else half,
        )

    def relay(k):
        for sign in (1, -1):

            @pl.when(reaches(-sign, k))
            def _():
                if k > 0:
                    landed(sign, k).wait_recv()
                if k + 1 < chips:

                    @pl.when(reaches(sign, 1))
                    def _():
                        hop(sign, k).start()

                if k > 0:
                    if square:
                        cross_back(sign, k).start()
                    hand_over(sign, k).start()

    def relay_half(k):
        for sign in (1, -1):

            @pl.when(reaches(-sign, k))
            def _():
                if k > 0:
                    half_landed(sign, k).wait_recv()
                if k + 1 < chips:

                    @pl.when(reaches(sign, 1))
                    def _():
                        half_hop(sign, k).start()

                if k > 0:
                    second(m, sign, k, 0).start()

    def share_cross(k):
        for sign in (1, -1):

            @pl.when(reaches(-sign, k))
            def _():
                cross_back(sign, k).wait_recv()
                second(m, sign, k, 1).start()

    def own_cross():
        return cross_copy(m, extra_send.at[0], extra_recv.at[0], 0, img_dev)

    def own_second(core):
        return x_copy(core, extra_send.at[1], extra_recv.at[1], sibling, 1)

    def send_table():
        return pltpu.make_async_remote_copy(
            table_out,
            table_in,
            extra_send.at[2],
            extra_recv.at[2],
            device_id=(m, across),
            device_id_type=MESH,
        )

    def send_scores():
        return pltpu.make_async_remote_copy(
            scores_out,
            scores_in,
            extra_send.at[3],
            extra_recv.at[3],
            device_id=(m, across),
            device_id_type=MESH,
        )

    relay(0)
    hand_over(1, 0).start()
    send_own(0)
    if square:
        own_cross().start()
        send_table().start()
        relay(1)
        for i in range(1, mine):
            send_own(i)
        own_cross().wait_recv()
        relay_half(0)
        own_second(m).start()
        pass_on(0)
        relay(2)
        relay_half(1)
        pass_on(1)
        for k in range(3, chips):
            relay(k)
        for i in range(2, mine):
            pass_on(i)
        send_table().wait_recv()
        read_table = pltpu.make_async_copy(table_in, table, local_sem.at[5])
        read_table.start()
        read_table.wait()
        relay_half(2)
    else:
        for i in range(1, mine):
            send_own(i)
        for k in range(1, chips):
            relay(k)
    def rest(early):
        if early:
            for k in range(3, chips):
                relay_half(k)
            share_cross(1)
            share_cross(2)
            return
        for k in range(3, chips):
            share_cross(k)
        keep_own()
        own_second(sibling).wait_recv()
        for k in range(1, chips):
            for sign in (1, -1):

                @pl.when(reaches(-sign, k))
                def _():
                    for piece in range(2):
                        second(sibling, sign, k, piece).wait_recv()

    def finish(base, number):
        count = number * padded
        logits = lax.dot_general(
            pooled[base : base + number].reshape(count, width),
            readout[...],
            (((1,), (1,)), ((), ())),
            preferred_element_type=F32,
        )
        classes = logits.shape[1]
        top = jnp.max(logits, axis=1, keepdims=True)
        total = top + jnp.log(jnp.sum(jnp.exp(logits - top), axis=1, keepdims=True))
        wanted = jnp.concatenate(
            [labels[i // steps][:, 0:1] for i in range(base, base + number)], axis=0
        )
        column = lax.broadcasted_iota(jnp.int32, (count, classes), 1)
        chosen = jnp.sum(jnp.where(column == wanted, logits, 0.0), axis=1, keepdims=True)
        kill = total - chosen
        row = lax.broadcasted_iota(jnp.int32, (count, 128), 0) % padded
        lane = lax.broadcasted_iota(jnp.int32, (count, 128), 1)
        return jnp.sum(
            jnp.where(row == lane, kill, 0.0).reshape(number, padded, 128), axis=1
        )

    def keep_own():
        spread = finish(0, mine * steps)
        for i in range(mine):
            kill_ref[first + i] = spread[i * steps : (i + 1) * steps, :surv]

    def build(i):
        for which in range(2):
            for place in range(1 if square else 0, len(origin)):
                arrived(which, i, place)
        for part in range(n_test):
            span = pl.ds(part * block, block)
            base1, delta1 = w1[span, :].astype(F32), d1_all[i, part].astype(F32)
            base2, delta2 = w2[:, span].astype(F32), d2_all[i, part].astype(F32)
            for step in range(steps):
                strength = strength_ref[step, first + i]
                w1_step[i, span, pl.ds(step * narrow, narrow)] = (
                    base1 + strength * delta1
                ).astype(BF16)
                w2_step[i, step, :, span] = (base2 + strength * delta2).astype(BF16)

    def variant(q, carry):
        i = q % mine
        if square:

            @pl.when(q == 1)
            def _():
                rest(True)

            @pl.when(q == mine)
            def _():
                rest(False)

        @pl.when((q > 0) & (q < mine))
        def _():
            build(i)

        def gather(held, entries, test):
            for j in range(surv):
                entry = entries[first + i, j]
                rows[pl.ds(j * slot, slot), :] = held[entry]
                number = (entry // img_dev * n_test + test) * img_dev + entry % img_dev
                labels[q, pl.ds(j, 1), :] = jnp.full(
                    (1, 128), label_ref[number], jnp.int32
                )

        @pl.when(q < mine)
        def _():
            gather(images, left_ref, t)

        if square:

            @pl.when(q >= mine)
            def _():
                gather(images2, table, across)

        hidden = jnp.maximum(
            jnp.dot(rows[...], w1_step[i], preferred_element_type=F32), 0.0
        ).astype(BF16)
        for low in range(0, width, narrow):
            span = pl.ds(low, narrow)
            residual = rows[:, span].astype(F32)
            for step in range(steps):
                out = jnp.maximum(
                    jnp.dot(
                        hidden[:, step * narrow : (step + 1) * narrow],
                        w2_step[i, step, :, span],
                        preferred_element_type=F32,
                    )
                    + residual,
                    0.0,
                )
                mean = jnp.sum(out.reshape(surv, slot, narrow), axis=1) * (1.0 / pix)
                pooled[q * steps + step, :, span] = jnp.concatenate(
                    [mean, jnp.zeros((padded - surv, narrow), F32)], axis=0
                ).astype(BF16)
        return carry

    for copy in local:
        copy.wait()
    build(0)
    handed(1, 0).wait_recv()
    for k in range(1, chips):
        for sign in (1, -1):

            @pl.when(reaches(-sign, k))
            def _():
                handed(sign, k).wait_recv()

    groups = mine * shards
    lax.fori_loop(0, groups, variant, 0)

    if square:
        scores_out[...] = finish(mine * steps, mine * steps)
        send_scores().start()
        send_scores().wait_recv()
        for i in range(mine):
            kill_ref[mine - first + i] = scores_in[i * steps : (i + 1) * steps, :surv]
    else:
        keep_own()

    hand_over(1, 0).wait_send()
    for k in range(chips):
        for sign in (1, -1):

            @pl.when(reaches(-sign, k))
            def _():
                if k > 0:
                    hand_over(sign, k).wait_send()
                if k + 1 < chips:

                    @pl.when(reaches(sign, 1))
                    def _():
                        hop(sign, k).wait_send()


    def drain(i, carry):
        for which in range(2):
            for place in range(len(near)):
                own_copy(which, i, place).wait_send()
            if square:
                held_copy(which, i, 0, along).wait_send()
        return carry

    lax.fori_loop(0, mine, drain, 0)
    if square:
        own_cross().wait_send()
        own_second(m).wait_send()
        send_table().wait_send()
        send_scores().wait_send()
        for k in range(chips):
            for sign in (1, -1):

                @pl.when(reaches(-sign, k))
                def _():
                    if k > 0:
                        cross_back(sign, k).wait_send()
                        second(m, sign, k, 0).wait_send()
                        second(m, sign, k, 1).wait_send()
                    if k + 1 < chips:

                        @pl.when(reaches(sign, 1))
                        def _():
                            half_hop(sign, k).wait_send()


def solution(mesh):
    n_mut, n_test = mesh.shape["mut"], mesh.shape["test"]

    def on_device(x, label, left, w1, w2, d1, d2, strength, readout):
        img_dev, pix, width = x.shape
        n_var, surv = left.shape
        steps = strength.shape[1]
        block, narrow = d1.shape[1], d1.shape[2]
        slot = round_up(pix, 16)
        padded = round_up(surv, 16)
        dma = pltpu.SemaphoreType.DMA
        places = max(3, n_test - 1)
        chips = n_mut // 2
        square = n_test == 4 and n_var == 4 and chips == 4
        mine = n_var // 2 if square else n_var
        groups = n_var
        smem = pl.BlockSpec(memory_space=pltpu.SMEM)
        vmem = pl.BlockSpec(memory_space=pltpu.VMEM)
        anywhere = pl.BlockSpec(memory_space=pltpu.HBM)
        macs = n_var * steps * surv * slot * width * narrow * 2
        return pl.pallas_call(
            functools.partial(kernel, n_mut, n_test),
            out_shape=jax.ShapeDtypeStruct((n_var, steps, surv), F32),
            in_specs=[smem, vmem, smem, smem, vmem] + [anywhere] * 5,
            out_specs=vmem,
            scratch_shapes=[
                pltpu.VMEM((n_mut * img_dev, slot, width), BF16),
                pltpu.VMEM((n_mut * img_dev, slot, width), BF16),
                pltpu.VMEM((mine, n_test, block, narrow), BF16),
                pltpu.VMEM((mine, n_test, narrow, block), BF16),
                pltpu.VMEM(w1.shape, BF16),
                pltpu.VMEM(w2.shape, BF16),
                pltpu.VMEM(readout.shape[::-1], BF16),
                pltpu.VMEM((surv * slot, width), BF16),
                pltpu.VMEM((mine, width, steps * narrow), BF16),
                pltpu.VMEM((mine, steps, narrow, width), BF16),
                pltpu.VMEM((groups * steps, padded, width), BF16),
                pltpu.VMEM((groups, padded, 128), jnp.int32),
                dma((6,)),
                dma((2, chips)),
                dma((2, chips)),
                dma((2, chips)),
                dma((2, chips)),
                dma((2, n_var, places)),
                dma((2, n_var, places)),
                dma((2, chips)),
                dma((2, chips)),
                dma((2, chips)),
                dma((2, chips)),
                dma((2, 2, chips)),
                dma((2, 2, chips)),
                dma((4,)),
                dma((4,)),
                pltpu.VMEM((round_up(n_var, 8), 128), jnp.int32),
                pltpu.VMEM((round_up(n_var, 8), 128), jnp.int32),
                pltpu.SMEM((round_up(n_var, 8), 128), jnp.int32),
                pltpu.VMEM((mine * steps, 128), F32),
                pltpu.VMEM((mine * steps, 128), F32),
            ],
            compiler_params=pltpu.CompilerParams(
                collective_id=0, has_side_effects=True, vmem_limit_bytes=60 * 2**20
            ),
            cost_estimate=pl.CostEstimate(
                flops=2 * macs, bytes_accessed=8 * 2**20, transcendentals=0
            ),
        )(left, left, strength.T, label, x.transpose(1, 0, 2), d1, d2, w1, w2, readout.T)

    return jax.shard_map(
        on_device,
        mesh=mesh,
        in_specs=(
            P(("mut", "test"), None, None),
            P(),
            P("mut", "test"),
            P(),
            P(),
            P("mut", "test", None),
            P("mut", None, "test"),
            P("mut", None),
            P(),
        ),
        out_specs=P("mut", None, "test"),
        check_vma=False,
    )
```
